128 devices in a mesh: row: 8 (over y, core), col: 16 (over x, z).
Axes of the slice: x: 4, y: 4, z: 4, core: 2. Of those that a mesh axis runs over, the one named last changes fastest.
Arguments:
- shares: bfloat16 [512, 16384], P('col', 'row'), may hold values from -6 to 6
- store: bfloat16 [16384, 65536], P('row', 'col'), may hold values from -0.046875 to 0.046875
- slot_query: int32 [512], replicated, may hold values from 0 to 511, each once
Outputs:
- answers: bfloat16 [512, 65536], P(('row', 'col'))
The draws below stay inside these ranges and needn't reach their ends.
Inputs may be any that keep to these rules, and one draw needn't show every extreme that they name: `slot_query`: a permutation: every slot names a different query.
All inputs are finite; a program needn't handle non-finite values.
Results may differ from the reference program's by a relative error of at most 0.015.
Values may be sent and summed in bfloat16 or wider, within the bound.
No kernel may reach another device: no remote copies, remote signals or barrier semaphores. Data moves between devices by JAX's collectives and lax.ppermute only.
A program may use at most 64 MiB of HBM per device.

```python
import jax
import jax.numpy as jnp
from jax import lax

C = 65536
ROWS_DEV = 2048
ROWS = 16384
QUERIES = 512


def with_spikes(entries, own_key, source, target, shards_of, factor):
    owner, partner = [(jnp.arange(entries.shape[axis_at]) // (entries.shape[axis_at] // shards_of)).reshape([-1 if axis == axis_at else 1 for axis in range(entries.ndim)]) for axis_at in (source, target)]
    chosen = jax.random.permutation(own_key, shards_of)[partner]
    strong = (owner == chosen) | (owner == (partner + shards_of // 2) % shards_of)
    return jnp.where(strong, factor * entries, entries)


def level_of(rng, shape, split, least, top_value):
    def one(dim, shards_of):
        steps = jax.random.uniform(jax.random.fold_in(jax.random.fold_in(rng, 6), dim), (shards_of,), jnp.float32, least / len(split), top_value / len(split))
        return jnp.repeat(jnp.exp(steps), shape[dim] // shards_of).reshape((-1,) + (1,) * (len(shape) - dim - 1))

    loudness = one(*split[0])
    for cut in split[1:]:
        loudness = loudness * one(*cut)
    return loudness


def gaussian(own_key, shape, width, reach, pieces=(), kind=jnp.bfloat16):
    entries = width * jax.random.normal(own_key, shape, jnp.float32)
    if pieces:
        entries = entries * level_of(own_key, shape, pieces, -0.22, 0.18)
    return jnp.clip(entries, -reach, reach).astype(kind)


def noise_with(rng, dims, deviation, bound, split, heavy, dtype=jnp.bfloat16):
    array = deviation * jax.random.normal(rng, dims, jnp.float32)
    if split:
        array = array * level_of(rng, dims, split, -0.22, 0.18)
    return jnp.clip(with_spikes(array, jax.random.fold_in(rng, 3), *heavy), -bound, bound).astype(dtype)


def setup_inputs(seed: int = 0) -> dict:
    keys = jax.random.split(jax.random.key(seed), 4)
    return {
        "shares": noise_with(keys[0], (QUERIES, ROWS), 1.0, 6.0, ((0, 16), (1, 8)), (1, 0, 16, 2.0)),
        "store": gaussian(keys[1], (ROWS, C), ROWS ** -0.5, 0.046875, ((0, 8), (1, 16))),
        "slot_query": jax.random.permutation(keys[2], QUERIES).astype(jnp.int32),
    }


def reference(shares, store, slot_query):
    chosen = jnp.take(shares, slot_query.astype(jnp.int32), axis=0)
    groups = ROWS // ROWS_DEV
    selected = chosen.reshape(QUERIES, groups, ROWS_DEV).transpose(1, 0, 2)
    blocks = store.reshape(groups, ROWS_DEV, C)

    def add_group(total, pair):
        part = jnp.dot(pair[0], pair[1], preferred_element_type=jnp.float32).astype(jnp.bfloat16)
        part = lax.optimization_barrier(part)
        return total + part.astype(jnp.float32), None

    total, _ = lax.scan(add_group, jnp.zeros((QUERIES, C), jnp.float32), (selected, blocks))
    return total.astype(jnp.bfloat16)
```

```python
import jax
import jax.numpy as jnp
from jax import lax
from jax.sharding import PartitionSpec as P

BOTH = ("row", "col")
CHUNKS = 2
HOPS = (0, 1, 3, 2)


def place(index):
    row, col = divmod(index, 16)
    return [col // 4, col % 4, row // 2, row % 2]


def moved(index, axis, hop, flip):
    at = place(index)
    at[axis] = at[axis] ^ flip if flip else (at[axis] + hop) % 4
    x, z, y, core = at
    return (y * 2 + core) * 16 + x * 4 + z


def send(value, axes, hop=0, flips=(0, 0)):
    pairs = []
    for index in range(128):
        core = place(index)[3]
        pairs.append((index, moved(index, axes[core], hop, flips[core])))
    return lax.ppermute(value, BOTH, pairs)


def to_other_core(value):
    pairs = [(index, index ^ 16) for index in range(128)]
    return lax.ppermute(value, BOTH, pairs)


def hop_of(j):
    return jnp.where(j == 2, 3, jnp.where(j == 3, 2, j))


def my_place():
    row, col = lax.axis_index("row"), lax.axis_index("col")
    return col // 4, col % 4, row // 2, row % 2


def slot_order():
    x, z, y, core = my_place()
    p = jnp.arange(512, dtype=jnp.int32)
    half, q1, q2, j1, j2, i = p // 256, p // 128 % 2, p // 64 % 2, p // 16 % 4, p // 4 % 4, p % 4
    owner = jnp.where(half == 0, core, 1 - core)
    first = owner == 0
    bits = jnp.where(first, q1 + 2 * q2, q2 + 2 * q1)
    gray = (y ^ (y // 2)) ^ bits
    to_y = gray ^ (gray // 2)
    to_x = (x + hop_of(jnp.where(first, j1, j2))) % 4
    to_z = (z + hop_of(jnp.where(first, j2, j1))) % 4
    return (to_y * 2 + owner) * 64 + (to_x * 4 + to_z) * 4 + i


def row_of_query(query):
    x, z, _, core = my_place()
    block = query // 32
    jx = hop_of((x - block // 4) % 4)
    jz = hop_of((z - block % 4) % 4)
    first, second = jnp.where(core == 0, jx, jz), jnp.where(core == 0, jz, jx)
    return (second * 4 + first) * 32 + query % 32


def gather_shares(shares):
    held = shares
    for axes in ((0, 1), (1, 0)):
        held = jnp.concatenate([held] + [send(held, axes, hop) for hop in HOPS[1:]], axis=0)
    return held


def add(a, b):
    return (a.astype(jnp.float32) + b.astype(jnp.float32)).astype(jnp.bfloat16)


def reduce_rows(part):
    held = add(part[:256], to_other_core(part[256:]))
    held = add(held[:128], send(held[128:], (2, 2), flips=(1, 3)))
    held = add(held[:64], send(held[64:], (2, 2), flips=(3, 1)))
    return held


def spread(held):
    width = held.shape[1]
    rows = held.reshape(4, 16, width)
    got = jnp.stack([rows[0]] + [send(rows[j], (0, 1), HOPS[j]) for j in (1, 2, 3)])
    rows = got.reshape(4, 4, 4, width)
    got = jnp.stack([rows[:, 0]] + [send(rows[:, j], (1, 0), HOPS[j]) for j in (1, 2, 3)])
    return got.reshape(16, 4, width)


def per_device(shares, store, slot_query):
    gathered = gather_shares(shares)
    query = jnp.take(slot_query, slot_order())
    pick = (row_of_query(query)[:, None] == jnp.arange(512)[None, :]).astype(jnp.bfloat16)
    chosen = jnp.dot(pick, gathered, preferred_element_type=jnp.float32).astype(jnp.bfloat16)
    width = store.shape[1] // CHUNKS
    pieces = []
    for k in range(CHUNKS):
        part = jnp.dot(chosen, store[:, k * width : (k + 1) * width], preferred_element_type=jnp.float32)
        pieces.append(spread(reduce_rows(part.astype(jnp.bfloat16))))
    x, z, _, core = my_place()
    source = jnp.arange(16, dtype=jnp.int32)
    jx, jz = hop_of((x - source // 4) % 4), hop_of((z - source % 4) % 4)
    at = jnp.where(core == 0, jz * 4 + jx, jx * 4 + jz)
    got = jnp.take(jnp.concatenate(pieces, axis=2), at, axis=0)
    return got.transpose(1, 0, 2).reshape(4, 65536)


def solution(mesh):
    return jax.shard_map(
        per_device,
        mesh=mesh,
        in_specs=(P("col", "row"), P("row", "col"), P()),
        out_specs=P(BOTH, None),
        check_vma=False,
    )
```

```python
import jax
import jax.numpy as jnp
from jax import lax
from jax.experimental import pallas as pl
from jax.experimental.pallas import tpu as pltpu
from jax.sharding import PartitionSpec as P

BOTH = ("row", "col")
WIDTHS = (2048, 2048)
TILE = 512
LOADS = 8
HOPS = (0, 1, 3, 2)


def place(index):
    row, col = divmod(index, 16)
    return [col // 4, col % 4, row // 2, row % 2]


def moved(index, axis, hop, flip):
    at = place(index)
    at[axis] = at[axis] ^ flip if flip else (at[axis] + hop) % 4
    x, z, y, core = at
    return (y * 2 + core) * 16 + x * 4 + z


def send(value, axes, hop=0, flips=(0, 0)):
    pairs = []
    for index in range(128):
        core = place(index)[3]
        pairs.append((index, moved(index, axes[core], hop, flips[core])))
    return lax.ppermute(value, BOTH, pairs)


def to_other_core(value):
    pairs = [(index, index ^ 16) for index in range(128)]
    return lax.ppermute(value, BOTH, pairs)


def hop_of(j):
    return jnp.where(j == 2, 3, jnp.where(j == 3, 2, j))


def my_place():
    row, col = lax.axis_index("row"), lax.axis_index("col")
    return col // 4, col % 4, row // 2, row % 2


def slot_order():
    _, _, y, core = my_place()
    p = jnp.arange(512, dtype=jnp.int32)
    half, q1, q2 = p // 256, p // 128 % 2, p // 64 % 2
    owner = jnp.where(half == 0, core, 1 - core)
    first = owner == 0
    bits = jnp.where(first, q1 + 2 * q2, q2 + 2 * q1)
    gray = (y ^ (y // 2)) ^ bits
    to_y = gray ^ (gray // 2)
    return (to_y * 2 + owner) * 64 + p % 64


def row_of_query(query):
    x, z, _, core = my_place()
    block = query // 32
    jx = hop_of((x - block // 4) % 4)
    jz = hop_of((z - block % 4) % 4)
    first, second = jnp.where(core == 0, jx, jz), jnp.where(core == 0, jz, jx)
    return (second * 4 + first) * 32 + query % 32


def gather_shares(shares):
    up, down, across = (send(shares, (0, 1), hop) for hop in HOPS[1:])
    low = jnp.concatenate([shares, up])
    high = jnp.concatenate([down, across])
    low_up, low_down = send(low, (1, 0), 1), send(low, (1, 0), 3)
    high_down, high_up = send(high, (1, 0), 3), send(high, (1, 0), 1)
    low_far, high_far = send(low_up, (1, 0), 1), send(high_down, (1, 0), 3)
    return [low, high, low_up, high_up, low_down, high_down, low_far, high_far]


def load_kernel(after_ref, store_ref, out_ref, sems):
    rows = store_ref.shape[0] // LOADS
    copies = []
    for k in range(LOADS):
        part = pl.ds(k * rows, rows)
        copies.append(pltpu.make_async_copy(store_ref.at[part], out_ref.at[part], sems.at[k]))
    for copy in copies:
        copy.start()
    for copy in copies:
        copy.wait()


def load(store, after):
    return pl.pallas_call(
        load_kernel,
        in_specs=[pl.BlockSpec(memory_space=pl.ANY), pl.BlockSpec(memory_space=pltpu.HBM)],
        out_specs=pl.BlockSpec(memory_space=pltpu.VMEM),
        out_shape=pltpu.VMEM(store.shape, store.dtype),
        scratch_shapes=[pltpu.SemaphoreType.DMA((LOADS,))],
        compiler_params=pltpu.CompilerParams(vmem_limit_bytes=42 * 2**20),
        cost_estimate=pl.CostEstimate(flops=0, bytes_accessed=2 * store.size * 2, transcendentals=0),
    )(after, store)


def choose_kernel(row_ref, *refs):
    *piece_refs, chosen_ref = refs
    lanes = lax.broadcasted_iota(jnp.int32, (512, 512), 1)
    pick = jnp.where(row_ref[...] == lanes, 1.0, 0.0).astype(jnp.bfloat16)
    for t in range(0, chosen_ref.shape[1], TILE):
        cols = slice(t, t + TILE)
        gathered = jnp.concatenate([ref[:, cols] for ref in piece_refs], axis=0)
        total = jnp.dot(pick, gathered, preferred_element_type=jnp.float32)
        chosen_ref[:, cols] = total.astype(jnp.bfloat16)


def choose(row, pieces):
    rows = pieces[0].shape[1]
    return pl.pallas_call(
        choose_kernel,
        in_specs=[pl.BlockSpec(memory_space=pltpu.VMEM)] * (1 + len(pieces)),
        out_specs=pl.BlockSpec(memory_space=pltpu.VMEM),
        out_shape=pltpu.VMEM((512, rows), jnp.bfloat16),
        compiler_params=pltpu.CompilerParams(vmem_limit_bytes=16 * 2**20),
        cost_estimate=pl.CostEstimate(
            flops=2 * 512 * 512 * rows, bytes_accessed=4 * 512 * rows, transcendentals=0
        ),
    )(row, *pieces)


def add(a, b):
    return (a.astype(jnp.float32) + b.astype(jnp.float32)).astype(jnp.bfloat16)


def reduce_rows(kept, sent):
    held = add(kept, to_other_core(sent))
    held = add(held[:128], send(held[128:], (2, 2), flips=(1, 3)))
    held = add(held[:64], send(held[64:], (2, 2), flips=(3, 1)))
    return held


def spread(held):
    rows = held.reshape(16, 4, held.shape[1])
    return lax.all_to_all(rows, "col", split_axis=0, concat_axis=0)


def per_device(shares, store, slot_query):
    pieces = gather_shares(shares)
    slot = jnp.arange(512, dtype=jnp.int32)
    row = jnp.where(slot_order()[:, None] == slot[None, :], row_of_query(slot_query)[None, :], 0)
    row = jnp.sum(row, axis=1, keepdims=True)
    store = load(store, pieces[1])
    chosen = choose(row, pieces)
    sums, start = [], 0
    for width in WIDTHS:
        part = jnp.dot(chosen, store[:, start : start + width], preferred_element_type=jnp.float32)
        part = part.astype(jnp.bfloat16)
        sums.append(reduce_rows(part[:256], part[256:]))
        start += width
    got = spread(jnp.concatenate(sums, axis=1))
    return got.transpose(1, 0, 2).reshape(4, 65536)


def solution(mesh):
    return jax.shard_map(
        per_device,
        mesh=mesh,
        in_specs=(P("col", "row"), P("row", "col"), P()),
        out_specs=P(BOTH, None),
        check_vma=False,
    )
```

```python
import jax
import jax.numpy as jnp
from jax import lax
from jax.experimental import pallas as pl
from jax.experimental.pallas import tpu as pltpu
from jax.sharding import PartitionSpec as P

BOTH = ("row", "col")
FIRST = 2048
PARTS = 4
TILE = 512
LOADS = 8
HOPS = (0, 1, 3, 2)


def place(index):
    row, col = divmod(index, 16)
    return [col // 4, col % 4, row // 2, row % 2]


def moved(index, axis, hop, flip):
    at = place(index)
    at[axis] = at[axis] ^ flip if flip else (at[axis] + hop) % 4
    x, z, y, core = at
    return (y * 2 + core) * 16 + x * 4 + z


def send(value, axes, hop=0, flips=(0, 0)):
    pairs = []
    for index in range(128):
        core = place(index)[3]
        pairs.append((index, moved(index, axes[core], hop, flips[core])))
    return lax.ppermute(value, BOTH, pairs)


def to_other_core(value):
    pairs = [(index, index ^ 16) for index in range(128)]
    return lax.ppermute(value, BOTH, pairs)


def hop_of(j):
    return jnp.where(j == 2, 3, jnp.where(j == 3, 2, j))


def my_place():
    row, col = lax.axis_index("row"), lax.axis_index("col")
    return col // 4, col % 4, row // 2, row % 2


def slot_order():
    _, _, y, core = my_place()
    p = jnp.arange(512, dtype=jnp.int32)
    half, q1, q2 = p // 256, p // 128 % 2, p // 64 % 2
    owner = jnp.where(half == 0, core, 1 - core)
    first = owner == 0
    bits = jnp.where(first, q1 + 2 * q2, q2 + 2 * q1)
    gray = (y ^ (y // 2)) ^ bits
    to_y = gray ^ (gray // 2)
    return (to_y * 2 + owner) * 64 + p % 64


def row_of_query(query):
    x, z, _, core = my_place()
    block = query // 32
    jx = hop_of((x - block // 4) % 4)
    jz = hop_of((z - block % 4) % 4)
    first, second = jnp.where(core == 0, jx, jz), jnp.where(core == 0, jz, jx)
    return (second * 4 + first) * 32 + query % 32


def gather_shares(shares, row):
    up, down, across = (send(shares, (0, 1), hop) for hop in HOPS[1:])
    low = jnp.concatenate([shares, up])
    high, row = lax.optimization_barrier((jnp.concatenate([down, across]), row))
    low_up, low_down = send(low, (1, 0), 1), send(low, (1, 0), 3)
    high_down, high_up = send(high, (1, 0), 3), send(high, (1, 0), 1)
    low_far, high_far = send(low_up, (1, 0), 1), send(high_down, (1, 0), 3)
    return [low, high, low_up, high_up, low_down, high_down, low_far, high_far], row


def load_kernel(after_ref, store_ref, out_ref, sems):
    rows = store_ref.shape[0] // LOADS
    copies = []
    for k in range(LOADS):
        part = pl.ds(k * rows, rows)
        copies.append(pltpu.make_async_copy(store_ref.at[part], out_ref.at[part], sems.at[k]))
    for copy in copies:
        copy.start()
    for copy in copies:
        copy.wait()


def load(store, after):
    return pl.pallas_call(
        load_kernel,
        in_specs=[pl.BlockSpec(memory_space=pl.ANY), pl.BlockSpec(memory_space=pltpu.HBM)],
        out_specs=pl.BlockSpec(memory_space=pltpu.VMEM),
        out_shape=pltpu.VMEM(store.shape, store.dtype),
        scratch_shapes=[pltpu.SemaphoreType.DMA((LOADS,))],
        compiler_params=pltpu.CompilerParams(vmem_limit_bytes=36 * 2**20),
        cost_estimate=pl.CostEstimate(flops=0, bytes_accessed=2 * store.size * 2, transcendentals=0),
    )(after, store)


def choose_kernel(row_ref, *refs):
    *piece_refs, chosen_ref = refs
    lanes = lax.broadcasted_iota(jnp.int32, (512, 512), 1)
    pick = jnp.where(row_ref[...] == lanes, 1.0, 0.0).astype(jnp.bfloat16)
    for t in range(0, chosen_ref.shape[1], TILE):
        cols = slice(t, t + TILE)
        gathered = jnp.concatenate([ref[:, cols] for ref in piece_refs], axis=0)
        total = jnp.dot(pick, gathered, preferred_element_type=jnp.float32)
        chosen_ref[:, cols] = total.astype(jnp.bfloat16)


def choose(row, pieces):
    rows = pieces[0].shape[1]
    return pl.pallas_call(
        choose_kernel,
        in_specs=[pl.BlockSpec(memory_space=pltpu.VMEM)] * (1 + len(pieces)),
        out_specs=pl.BlockSpec(memory_space=pltpu.VMEM),
        out_shape=pltpu.VMEM((512, rows), jnp.bfloat16),
        compiler_params=pltpu.CompilerParams(vmem_limit_bytes=16 * 2**20),
        cost_estimate=pl.CostEstimate(
            flops=2 * 512 * 512 * rows, bytes_accessed=4 * 512 * rows, transcendentals=0
        ),
    )(row, *pieces)


def add(a, b):
    return (a.astype(jnp.float32) + b.astype(jnp.float32)).astype(jnp.bfloat16)


def product(chosen, store):
    return jnp.dot(chosen, store, preferred_element_type=jnp.float32).astype(jnp.bfloat16)


def sum_y(held):
    held = add(held[:128], send(held[128:], (2, 2), flips=(1, 3)))
    return add(held[:64], send(held[64:], (2, 2), flips=(3, 1)))


def spread(held):
    rows = held.reshape(16, 4, held.shape[1])
    return lax.all_to_all(rows, "col", split_axis=0, concat_axis=0)


def per_device(shares, store, slot_query):
    slot = jnp.arange(512, dtype=jnp.int32)
    row = jnp.where(slot_order()[:, None] == slot[None, :], row_of_query(slot_query)[None, :], 0)
    row = jnp.sum(row, axis=1, keepdims=True)
    pieces, row = gather_shares(shares, row)
    store = load(store, pieces[1])
    chosen = choose(row, pieces)
    sums = []
    for part in (store[:, :FIRST], store[:, FIRST:]):
        part = product(chosen, part)
        sums.append(sum_y(add(part[:256], to_other_core(part[256:]))))
    got = spread(jnp.concatenate(sums, axis=1))
    return got.transpose(1, 0, 2).reshape(4, 65536)


def solution(mesh):
    return jax.shard_map(
        per_device,
        mesh=mesh,
        in_specs=(P("col", "row"), P("row", "col"), P()),
        out_specs=P(BOTH, None),
        check_vma=False,
    )
```

```python
import functools

import jax
import jax.numpy as jnp
from jax import lax
from jax.experimental import pallas as pl
from jax.experimental.pallas import tpu as pltpu
from jax.sharding import PartitionSpec as P

BOTH = ("row", "col")
WIDTHS = (3072, 1024)
TILE = 512
LIMIT = 14 * 2**20
EARLY_LIMIT = 34 * 2**20
LOADS = 4
IN_VMEM = pl.BlockSpec(memory_space=pltpu.VMEM)
HOPS = (0, 1, 3, 2)


def place(index):
    row, col = divmod(index, 16)
    return [col // 4, col % 4, row // 2, row % 2]


def moved(index, axis, hop, flip):
    at = place(index)
    at[axis] = at[axis] ^ flip if flip else (at[axis] + hop) % 4
    x, z, y, core = at
    return (y * 2 + core) * 16 + x * 4 + z


def send(value, axes, hop=0, flips=(0, 0)):
    pairs = []
    for index in range(128):
        core = place(index)[3]
        pairs.append((index, moved(index, axes[core], hop, flips[core])))
    return lax.ppermute(value, BOTH, pairs)


def to_other_core(value):
    pairs = [(index, index ^ 16) for index in range(128)]
    return lax.ppermute(value, BOTH, pairs)


def hop_of(j):
    return jnp.where(j == 2, 3, jnp.where(j == 3, 2, j))


def my_place():
    row, col = lax.axis_index("row"), lax.axis_index("col")
    return col // 4, col % 4, row // 2, row % 2


def slot_order():
    _, _, y, core = my_place()
    p = jnp.arange(512, dtype=jnp.int32)
    half, q1, q2 = p // 256, p // 128 % 2, p // 64 % 2
    owner = jnp.where(half == 0, core, 1 - core)
    first = owner == 0
    bits = jnp.where(first, q1 + 2 * q2, q2 + 2 * q1)
    gray = (y ^ (y // 2)) ^ bits
    to_y = gray ^ (gray // 2)
    return (to_y * 2 + owner) * 64 + p % 64


def row_of_query(query):
    x, z, _, core = my_place()
    block = query // 32
    jx = hop_of((x - block // 4) % 4)
    jz = hop_of((z - block % 4) % 4)
    first, second = jnp.where(core == 0, jx, jz), jnp.where(core == 0, jz, jx)
    piece = second * 2 + first // 2
    piece = jnp.where(piece == 3, 4, jnp.where(piece == 4, 5, jnp.where(piece == 5, 3, piece)))
    return piece * 64 + first % 2 * 32 + query % 32


def gather_shares(shares, row):
    up, down, across = (send(shares, (0, 1), hop) for hop in HOPS[1:])
    low = jnp.concatenate([shares, up])
    high, row = lax.optimization_barrier((jnp.concatenate([down, across]), row))
    low_up, low_down = send(low, (1, 0), 1), send(low, (1, 0), 3)
    high_down, high_up = send(high, (1, 0), 3), send(high, (1, 0), 1)
    low_far, high_far = send(low_up, (1, 0), 1), send(high_down, (1, 0), 3)
    return [low, high, low_up, high_down, high_up, low_down, low_far, high_far], row


def columns(start, width):
    return slice(start, start + width)


def early_kernel(*refs):
    *piece_refs, store_ref, out_ref, held_ref, total_ref, sems = refs
    depth = store_ref.shape[0] // LOADS
    copies = []
    for k in range(LOADS):
        at = pl.ds(k * depth, depth)
        copies.append(pltpu.make_async_copy(store_ref.at[at], held_ref.at[at], sems.at[k]))
        copies[k].start()
    for k in range(LOADS):
        at = columns(k * depth, depth)
        left = jnp.concatenate([ref[:, at] for ref in piece_refs], axis=0)
        copies[k].wait()
        for t in range(0, out_ref.shape[1], TILE):
            to = columns(t, TILE)
            part = jnp.dot(left, held_ref[at, to], preferred_element_type=jnp.float32)
            if k > 0:
                part += total_ref[:, to]
            if k < LOADS - 1:
                total_ref[:, to] = part
            else:
                out_ref[:, to] = part.astype(jnp.bfloat16)


def early_product(pieces, store):
    count = sum(piece.shape[0] for piece in pieces)
    rows, width = store.shape
    return pl.pallas_call(
        early_kernel,
        in_specs=[IN_VMEM] * len(pieces) + [pl.BlockSpec(memory_space=pltpu.HBM)],
        out_specs=[IN_VMEM] * 2,
        out_shape=[pltpu.VMEM((count, width), jnp.bfloat16), pltpu.VMEM(store.shape, store.dtype)],
        scratch_shapes=[pltpu.VMEM((count, width), jnp.float32), pltpu.SemaphoreType.DMA((LOADS,))],
        compiler_params=pltpu.CompilerParams(vmem_limit_bytes=EARLY_LIMIT),
        cost_estimate=pl.CostEstimate(
            flops=2 * count * rows * width, bytes_accessed=2 * rows * width, transcendentals=0
        ),
    )(*pieces, store)


def late_kernel(start, row_ref, *refs):
    *piece_refs, early_ref, store_ref, kept_ref, sent_ref = refs
    lanes = lax.broadcasted_iota(jnp.int32, (512, 512), 1)
    pick = jnp.where(row_ref[...] == lanes, 1.0, 0.0).astype(jnp.bfloat16)
    held = jnp.concatenate([ref[...] for ref in piece_refs], axis=0)
    for t in range(0, kept_ref.shape[1], TILE):
        at = columns(start + t, TILE)
        part = jnp.dot(held, store_ref[:, at], preferred_element_type=jnp.float32).astype(jnp.bfloat16)
        both = jnp.concatenate([early_ref[:, at], part], axis=0)
        part = jnp.dot(pick, both, preferred_element_type=jnp.float32).astype(jnp.bfloat16)
        kept_ref[:, columns(t, TILE)] = part[:256]
        sent_ref[:, columns(t, TILE)] = part[256:]


def late_product(row, pieces, early, store, start, width):
    rows = store.shape[0]
    return pl.pallas_call(
        functools.partial(late_kernel, start),
        in_specs=[IN_VMEM] * (len(pieces) + 3),
        out_specs=[IN_VMEM] * 2,
        out_shape=[pltpu.VMEM((256, width), jnp.bfloat16)] * 2,
        compiler_params=pltpu.CompilerParams(vmem_limit_bytes=LIMIT),
        cost_estimate=pl.CostEstimate(
            flops=2 * 256 * (rows + 1024) * width, bytes_accessed=2 * rows * width, transcendentals=0
        ),
    )(row, *pieces, early, store)


def add(a, b):
    return (a.astype(jnp.float32) + b.astype(jnp.float32)).astype(jnp.bfloat16)


def product(chosen, store):
    return jnp.dot(chosen, store, preferred_element_type=jnp.float32).astype(jnp.bfloat16)


def sum_y(held):
    held = add(held[:128], send(held[128:], (2, 2), flips=(1, 3)))
    return add(held[:64], send(held[64:], (2, 2), flips=(3, 1)))


def spread(held):
    rows = held.reshape(16, 4, held.shape[1])
    return lax.all_to_all(rows, "col", split_axis=0, concat_axis=0)


def per_device(shares, store, slot_query):
    slot = jnp.arange(512, dtype=jnp.int32)
    row = jnp.where(slot_order()[:, None] == slot[None, :], row_of_query(slot_query)[None, :], 0)
    row = jnp.sum(row, axis=1, keepdims=True)
    pieces, row = gather_shares(shares, row)
    early, store = early_product(pieces[:4], store)
    sums, start = [], 0
    for width in WIDTHS:
        kept, sent = late_product(row, pieces[4:], early, store, start, width)
        sums.append(sum_y(add(kept, to_other_core(sent))))
        start += width
    got = spread(jnp.concatenate(sums, axis=1))
    return got.transpose(1, 0, 2).reshape(4, 65536)


def solution(mesh):
    return jax.shard_map(
        per_device,
        mesh=mesh,
        in_specs=(P("col", "row"), P("row", "col"), P()),
        out_specs=P(BOTH, None),
        check_vma=False,
    )
```

```python
import functools

import jax
import jax.numpy as jnp
from jax import lax
from jax.experimental import pallas as pl
from jax.experimental.pallas import tpu as pltpu
from jax.sharding import PartitionSpec as P

BOTH = ("row", "col")
WIDTHS = (3072, 1024)
TILE = 512
LIMIT = 14 * 2**20
EARLY_LIMIT = 34 * 2**20
LOADS = 4
IN_VMEM = pl.BlockSpec(memory_space=pltpu.VMEM)
HOPS = (0, 1, 3, 2)


def place(index):
    row, col = divmod(index, 16)
    return [col // 4, col % 4, row // 2, row % 2]


def moved(index, axis, hop, flip):
    at = place(index)
    at[axis] = at[axis] ^ flip if flip else (at[axis] + hop) % 4
    x, z, y, core = at
    return (y * 2 + core) * 16 + x * 4 + z


def send(value, axes, hop=0, flips=(0, 0)):
    pairs = []
    for index in range(128):
        core = place(index)[3]
        pairs.append((index, moved(index, axes[core], hop, flips[core])))
    return lax.ppermute(value, BOTH, pairs)


def to_other_core(value):
    pairs = [(index, index ^ 16) for index in range(128)]
    return lax.ppermute(value, BOTH, pairs)


def my_place():
    row, col = lax.axis_index("row"), lax.axis_index("col")
    return col >> 2, col & 3, row >> 1, row & 1


def slot_order():
    _, _, y, core = my_place()
    p = lax.broadcasted_iota(jnp.int32, (512, 1), 0)
    half, q1, q2 = p >> 8, (p >> 7) & 1, (p >> 6) & 1
    owner = half ^ core
    bits = jnp.where(owner == 0, q1 + 2 * q2, q2 + 2 * q1)
    gray = bits ^ (y ^ (y >> 1))
    to_y = gray ^ (gray >> 1)
    return (to_y * 2 + owner) * 64 + (p & 63)


def row_of_query(query):
    x, z, _, core = my_place()
    jx, jz = (x - (query >> 7)) & 3, (z - ((query >> 5) & 3)) & 3
    jx, jz = jx ^ (jx >> 1), jz ^ (jz >> 1)
    first, second = jx + core * (jz - jx), jz + core * (jx - jz)
    piece = second * 2 + (first >> 1)
    piece = jnp.where(piece == 3, 4, jnp.where(piece == 4, 3, piece))
    return piece * 64 + (first & 1) * 32 + (query & 31)


def gather_shares(shares):
    up, down, across = (send(shares, (0, 1), hop) for hop in HOPS[1:])
    low = jnp.concatenate([shares, up])
    high = jnp.concatenate([down, across])
    low_up, low_down = send(low, (1, 0), 1), send(low, (1, 0), 3)
    low, high = lax.optimization_barrier((low, high))
    far = send(jnp.concatenate([low, high]), (1, 0), 2)
    high_up, high_down = send(high, (1, 0), 1), send(high, (1, 0), 3)
    return [low, high, low_up, low_down, high_up, high_down, far]


def columns(start, width):
    return slice(start, start + width)


def early_kernel(*refs):
    query_ref, *piece_refs, store_ref, row_ref, out_ref, held_ref, total_ref, sems = refs
    depth = store_ref.shape[0] // LOADS
    copies = []
    for k in range(LOADS):
        at = pl.ds(k * depth, depth)
        copies.append(pltpu.make_async_copy(store_ref.at[at], held_ref.at[at], sems.at[k]))
        copies[k].start()
    lanes = lax.broadcasted_iota(jnp.int32, (512, 512), 1)
    row = jnp.where(slot_order() == lanes, row_of_query(query_ref[...]).astype(jnp.float32), 0.0)
    row_ref[...] = jnp.sum(row, axis=1, keepdims=True).astype(jnp.int32)
    for k in range(LOADS):
        at = columns(k * depth, depth)
        left = jnp.concatenate([ref[:, at] for ref in piece_refs], axis=0)
        copies[k].wait()
        for t in range(0, out_ref.shape[1], TILE):
            to = columns(t, TILE)
            part = jnp.dot(left, held_ref[at, to], preferred_element_type=jnp.float32)
            if k > 0:
                part += total_ref[:, to]
            if k < LOADS - 1:
                total_ref[:, to] = part
            else:
                out_ref[:, to] = part.astype(jnp.bfloat16)


def early_product(slot_query, pieces, store):
    count = sum(piece.shape[0] for piece in pieces)
    rows, width = store.shape
    return pl.pallas_call(
        early_kernel,
        in_specs=[IN_VMEM] * (1 + len(pieces)) + [pl.BlockSpec(memory_space=pltpu.HBM)],
        out_specs=[IN_VMEM] * 3,
        out_shape=[
            pltpu.VMEM((512, 1), jnp.int32),
            pltpu.VMEM((count, width), jnp.bfloat16),
            pltpu.VMEM(store.shape, store.dtype),
        ],
        scratch_shapes=[pltpu.VMEM((count, width), jnp.float32), pltpu.SemaphoreType.DMA((LOADS,))],
        compiler_params=pltpu.CompilerParams(vmem_limit_bytes=EARLY_LIMIT),
        cost_estimate=pl.CostEstimate(
            flops=2 * count * rows * width, bytes_accessed=2 * rows * width, transcendentals=0
        ),
    )(slot_query.reshape(1, 512), *pieces, store)


def late_kernel(start, row_ref, *refs):
    *piece_refs, early_ref, store_ref, kept_ref, sent_ref = refs
    lanes = lax.broadcasted_iota(jnp.int32, (512, 512), 1)
    pick = jnp.where(row_ref[...] == lanes, 1.0, 0.0).astype(jnp.bfloat16)
    held = jnp.concatenate([ref[...] for ref in piece_refs], axis=0)
    for t in range(0, kept_ref.shape[1], TILE):
        at = columns(start + t, TILE)
        part = jnp.dot(held, store_ref[:, at], preferred_element_type=jnp.float32).astype(jnp.bfloat16)
        both = jnp.concatenate([early_ref[:, at], part], axis=0)
        part = jnp.dot(pick, both, preferred_element_type=jnp.float32).astype(jnp.bfloat16)
        kept_ref[:, columns(t, TILE)] = part[:256]
        sent_ref[:, columns(t, TILE)] = part[256:]


def late_product(row, pieces, early, store, start, width):
    rows = store.shape[0]
    return pl.pallas_call(
        functools.partial(late_kernel, start),
        in_specs=[IN_VMEM] * (len(pieces) + 3),
        out_specs=[IN_VMEM] * 2,
        out_shape=[pltpu.VMEM((256, width), jnp.bfloat16)] * 2,
        compiler_params=pltpu.CompilerParams(vmem_limit_bytes=LIMIT),
        cost_estimate=pl.CostEstimate(
            flops=2 * 256 * (rows + 1024) * width, bytes_accessed=2 * rows * width, transcendentals=0
        ),
    )(row, *pieces, early, store)


def add(a, b):
    return (a.astype(jnp.float32) + b.astype(jnp.float32)).astype(jnp.bfloat16)


def product(chosen, store):
    return jnp.dot(chosen, store, preferred_element_type=jnp.float32).astype(jnp.bfloat16)


def sum_y(held):
    held = add(held[:128], send(held[128:], (2, 2), flips=(1, 3)))
    return add(held[:64], send(held[64:], (2, 2), flips=(3, 1)))


def spread(held):
    rows = held.reshape(16, 4, held.shape[1])
    return lax.all_to_all(rows, "col", split_axis=0, concat_axis=0)


def per_device(shares, store, slot_query):
    pieces = gather_shares(shares)
    row, early, store = early_product(slot_query, pieces[:4], store)
    sums, start = [], 0
    for width in WIDTHS:
        kept, sent = late_product(row, pieces[4:], early, store, start, width)
        sums.append(sum_y(add(kept, to_other_core(sent))))
        start += width
    got = spread(jnp.concatenate(sums, axis=1))
    return got.transpose(1, 0, 2).reshape(4, 65536)


def solution(mesh):
    return jax.shard_map(
        per_device,
        mesh=mesh,
        in_specs=(P("col", "row"), P("row", "col"), P()),
        out_specs=P(BOTH, None),
        check_vma=False,
    )
```

```python
import functools

import jax
import jax.numpy as jnp
from jax import lax
from jax.experimental import pallas as pl
from jax.experimental.pallas import tpu as pltpu
from jax.sharding import PartitionSpec as P

BOTH = ("row", "col")
WIDTHS = (3072, 1024)
TILE = 512
LIMIT = 14 * 2**20
EARLY_LIMIT = 32 * 2**20
LOADS = 8
IN_VMEM = pl.BlockSpec(memory_space=pltpu.VMEM)
HOPS = (0, 1, 3, 2)


def place(index):
    row, col = divmod(index, 16)
    return [col // 4, col % 4, row // 2, row % 2]


def moved(index, axis, hop, flip):
    at = place(index)
    at[axis] = at[axis] ^ flip if flip else (at[axis] + hop) % 4
    x, z, y, core = at
    return (y * 2 + core) * 16 + x * 4 + z


def send(value, axes, hop=0, flips=(0, 0)):
    pairs = []
    for index in range(128):
        core = place(index)[3]
        pairs.append((index, moved(index, axes[core], hop, flips[core])))
    return lax.ppermute(value, BOTH, pairs)


def to_other_core(value):
    pairs = [(index, index ^ 16) for index in range(128)]
    return lax.ppermute(value, BOTH, pairs)


def my_place():
    row, col = lax.axis_index("row"), lax.axis_index("col")
    return col >> 2, col & 3, row >> 1, row & 1


def slot_order():
    _, _, y, core = my_place()
    p = lax.broadcasted_iota(jnp.int32, (512, 1), 0)
    half, q1, q2 = p >> 8, (p >> 7) & 1, (p >> 6) & 1
    owner = half ^ core
    bits = jnp.where(owner == 0, q1 + 2 * q2, q2 + 2 * q1)
    gray = bits ^ (y ^ (y >> 1))
    to_y = gray ^ (gray >> 1)
    return (to_y * 2 + owner) * 64 + (p & 63)


def row_of_query(query):
    x, z, _, core = my_place()
    jx, jz = (x - (query >> 7)) & 3, (z - ((query >> 5) & 3)) & 3
    jx, jz = jx ^ (jx >> 1), jz ^ (jz >> 1)
    first, second = jx + core * (jz - jx), jz + core * (jx - jz)
    piece = second * 2 + (first >> 1)
    piece = jnp.where(piece == 3, 4, jnp.where(piece == 4, 3, piece))
    return piece * 64 + (first & 1) * 32 + (query & 31)


def gather_shares(shares):
    up, down, across = (send(shares, (0, 1), hop) for hop in HOPS[1:])
    low = jnp.concatenate([shares, up])
    high = jnp.concatenate([down, across])
    low_up, low_down = send(low, (1, 0), 1), send(low, (1, 0), 3)
    low, high = lax.optimization_barrier((low, high))
    far = send(jnp.concatenate([low, high]), (1, 0), 2)
    high_up, high_down = send(high, (1, 0), 1), send(high, (1, 0), 3)
    return [low, high, low_up, low_down, high_up, high_down, far]


def columns(start, width):
    return slice(start, start + width)


def early_kernel(*refs):
    query_ref, *piece_refs, store_ref, row_ref, out_ref, held_ref, total_ref, sems = refs
    depth = store_ref.shape[0] // LOADS
    copies = []
    for k in range(LOADS):
        at = pl.ds(k * depth, depth)
        copies.append(pltpu.make_async_copy(store_ref.at[at], held_ref.at[at], sems.at[k]))
        copies[k].start()
    lanes = lax.broadcasted_iota(jnp.int32, (512, 512), 1)
    row = jnp.where(slot_order() == lanes, row_of_query(query_ref[...]).astype(jnp.float32), 0.0)
    row_ref[...] = jnp.sum(row, axis=1, keepdims=True).astype(jnp.int32)
    for k in range(LOADS):
        at = columns(k * depth, depth)
        left = jnp.concatenate([ref[:, at] for ref in piece_refs], axis=0)
        copies[k].wait()
        for t in range(0, out_ref.shape[1], TILE):
            to = columns(t, TILE)
            part = jnp.dot(left, held_ref[at, to], preferred_element_type=jnp.float32)
            if k > 0:
                part += total_ref[:, to]
            if k < LOADS - 1:
                total_ref[:, to] = part
            else:
                out_ref[:, to] = part.astype(jnp.bfloat16)


def early_product(slot_query, pieces, store):
    count = sum(piece.shape[0] for piece in pieces)
    rows, width = store.shape
    return pl.pallas_call(
        early_kernel,
        in_specs=[IN_VMEM] * (1 + len(pieces)) + [pl.BlockSpec(memory_space=pltpu.HBM)],
        out_specs=[IN_VMEM] * 3,
        out_shape=[
            pltpu.VMEM((512, 1), jnp.int32),
            pltpu.VMEM((count, width), jnp.bfloat16),
            pltpu.VMEM(store.shape, store.dtype),
        ],
        scratch_shapes=[pltpu.VMEM((count, width), jnp.float32), pltpu.SemaphoreType.DMA((LOADS,))],
        compiler_params=pltpu.CompilerParams(vmem_limit_bytes=EARLY_LIMIT),
        cost_estimate=pl.CostEstimate(
            flops=2 * count * rows * width, bytes_accessed=2 * rows * width, transcendentals=0
        ),
    )(slot_query.reshape(1, 512), *pieces, store)


def late_kernel(start, row_ref, *refs):
    *piece_refs, early_ref, store_ref, kept_ref, sent_ref = refs
    lanes = lax.broadcasted_iota(jnp.int32, (512, 512), 1)
    pick = jnp.where(row_ref[...] == lanes, 1.0, 0.0).astype(jnp.bfloat16)
    held = jnp.concatenate([ref[...] for ref in piece_refs], axis=0)
    for t in range(0, kept_ref.shape[1], TILE):
        at = columns(start + t, TILE)
        part = jnp.dot(held, store_ref[:, at], preferred_element_type=jnp.float32).astype(jnp.bfloat16)
        both = jnp.concatenate([early_ref[:, at], part], axis=0)
        part = jnp.dot(pick, both, preferred_element_type=jnp.float32).astype(jnp.bfloat16)
        kept_ref[:, columns(t, TILE)] = part[:256]
        sent_ref[:, columns(t, TILE)] = part[256:]


def late_product(row, pieces, early, store, start, width):
    rows = store.shape[0]
    return pl.pallas_call(
        functools.partial(late_kernel, start),
        in_specs=[IN_VMEM] * (len(pieces) + 3),
        out_specs=[IN_VMEM] * 2,
        out_shape=[pltpu.VMEM((256, width), jnp.bfloat16)] * 2,
        compiler_params=pltpu.CompilerParams(vmem_limit_bytes=LIMIT),
        cost_estimate=pl.CostEstimate(
            flops=2 * 256 * (rows + 1024) * width, bytes_accessed=2 * rows * width, transcendentals=0
        ),
    )(row, *pieces, early, store)


def add(a, b):
    return (a.astype(jnp.float32) + b.astype(jnp.float32)).astype(jnp.bfloat16)


def product(chosen, store):
    return jnp.dot(chosen, store, preferred_element_type=jnp.float32).astype(jnp.bfloat16)


def sum_y(held):
    held = add(held[:128], send(held[128:], (2, 2), flips=(1, 3)))
    return add(held[:64], send(held[64:], (2, 2), flips=(3, 1)))


def spread(held):
    rows = held.reshape(16, 4, held.shape[1])
    return lax.all_to_all(rows, "col", split_axis=0, concat_axis=0)


def per_device(shares, store, slot_query):
    pieces = gather_shares(shares)
    row, early, store = early_product(slot_query, pieces[:4], store)
    sums, start = [], 0
    for width in WIDTHS:
        kept, sent = late_product(row, pieces[4:], early, store, start, width)
        sums.append(sum_y(add(kept, to_other_core(sent))))
        start += width
    got = spread(jnp.concatenate(sums, axis=1))
    return got.transpose(1, 0, 2).reshape(4, 65536)


def solution(mesh):
    return jax.shard_map(
        per_device,
        mesh=mesh,
        in_specs=(P("col", "row"), P("row", "col"), P()),
        out_specs=P(BOTH, None),
        check_vma=False,
    )
```
